32 devices in a mesh: heads: 4 (over z), seq: 8 (over y, x, core).
Axes of the slice: x: 2, y: 2, z: 4, core: 2. Of those that a mesh axis runs over, the one named last changes fastest.
Arguments:
- frames: bfloat16 [8, 1024, 1152], P('seq', None, 'heads'), may hold values from -6 to 6
- qkv_spatial: bfloat16 [3, 1152, 1152], P(None, None, 'heads'), may hold values from -1 to 1
- out_spatial: bfloat16 [1152, 1152], P('heads'), may hold values from -0.1875 to 0.1875
- qkv_temporal: bfloat16 [3, 1152, 1152], P(None, None, 'heads'), may hold values from -1 to 1
- out_temporal: bfloat16 [1152, 1152], P('heads'), may hold values from -0.1875 to 0.1875
- spatial_mask: int32 [8, 8, 8], P('seq'), may hold values from 0 to 1
- temporal_mask: int32 [8, 8, 8], replicated, may hold values 0 or 1
- cotangent: bfloat16 [8, 1024, 1152], P(None, 'seq', 'heads'), may hold values from -6 to 6
Outputs:
- result: bfloat16 [8, 1024, 1152], P(None, 'seq', 'heads')
- frames_grad: bfloat16 [8, 1024, 1152], P('seq', None, 'heads')
- spatial_qkv_grad: float32 [3, 1152, 1152], P(None, 'seq', 'heads')
- spatial_out_grad: float32 [1152, 1152], P('heads', 'seq')
- temporal_qkv_grad: float32 [3, 1152, 1152], P(None, 'seq', 'heads')
- temporal_out_grad: float32 [1152, 1152], P('heads', 'seq')
The draws below stay inside these ranges and needn't reach their ends.
All inputs are finite; a program needn't handle non-finite values.
Results may differ from the reference program's by a relative error of at most 0.018.
Values may be sent and summed in bfloat16 or wider, within the bound.
A program may use at most 192 MiB of HBM per device.

```python
import jax
import jax.numpy as jnp
from jax import lax

D = 1152
HEADS = 16
HEAD_SIZE = 72
P_SIZE = 1024
BLK = 128
FRAMES = 8
NB = 8


def weight_stack(key):
    pieces = jax.random.split(key, 3)
    base_part = jax.random.normal(pieces[0], (D, D), jnp.float32)
    own_part = jax.random.normal(pieces[1], (D, D), jnp.float32)
    value_part = jax.random.normal(pieces[2], (D, D), jnp.float32)
    stacked = jnp.stack([base_part, own_part, value_part]) * D ** (-0.5)
    return jnp.clip(stacked, -1.0, 1.0)


def draw_qkv_spatial(key, part):
    key = jax.random.fold_in(key, 5)
    return weight_stack(key).astype(jnp.bfloat16)


def draw_qkv_temporal(key, part):
    key = jax.random.fold_in(key, 9)
    return weight_stack(key).astype(jnp.bfloat16)


def draw_spatial_mask(key, part):
    key = jax.random.fold_in(key, 13)
    first_key, second_key = jax.random.split(key)
    levels = jax.random.randint(first_key, (FRAMES, 1, 1), 1, 5)
    rolled = jax.random.randint(second_key, (FRAMES, NB, NB), 0, 4)
    return (rolled < levels).astype(jnp.int32)


def with_ends(entries, stream_key, least, high):
    shape = entries.shape
    place = [jax.random.randint(jax.random.fold_in(stream_key, axis), (), 0, shape[axis]) for axis in range(len(shape))]
    entries = entries.at[tuple(place)].set(least)
    longest = shape.index(max(shape))
    place[longest] = (place[longest] + 1) % shape[longest]
    return entries.at[tuple(place)].set(high)


def block_levels(own_key, shape, cuts, least, top_value):
    def one(dim, parts):
        heights = jax.random.uniform(jax.random.fold_in(jax.random.fold_in(own_key, 6), dim), (parts,), jnp.float32, least / len(cuts), top_value / len(cuts))
        return jnp.repeat(jnp.exp(heights), shape[dim] // parts).reshape((-1,) + (1,) * (len(shape) - dim - 1))

    loudness = one(*cuts[0])
    for cut in cuts[1:]:
        loudness = loudness * one(*cut)
    return loudness


def normal_values(key, dims, width, most, cuts=(), kind=jnp.bfloat16):
    factor_of = block_levels(key, dims, cuts, -0.22, 0.18) if cuts else 1.0
    array = jax.random.normal(key, dims, jnp.float32) * width * factor_of
    return jnp.minimum(jnp.maximum(array, -most), most).astype(kind)


def setup_inputs(seed: int = 0) -> dict:
    streams_of = jax.random.split(jax.random.key(seed), 9)
    frames = normal_values(streams_of[0], (FRAMES, P_SIZE, D), 1.0, 6.0, ((0, 8), (2, 4)))
    qkv_spatial = draw_qkv_spatial(jax.random.fold_in(streams_of[8], 71), 0)
    out_spatial = normal_values(streams_of[2], (D, D), D ** -0.5, 0.1875, ((0, 4),))
    qkv_temporal = draw_qkv_temporal(jax.random.fold_in(streams_of[8], 71), 0)
    out_temporal = normal_values(streams_of[4], (D, D), D ** -0.5, 0.1875, ((0, 4),))
    spatial_mask = draw_spatial_mask(jax.random.fold_in(streams_of[8], 71), 0)
    temporal_mask = with_ends((jax.random.randint(streams_of[6], (NB, FRAMES, FRAMES), 0, 4) < 3).astype(jnp.int32), jax.random.fold_in(streams_of[6], 1), 0, 1)
    cotangent = normal_values(streams_of[7], (FRAMES, P_SIZE, D), 1.0, 6.0, ((1, 8), (2, 4)))
    return {"frames": frames, "qkv_spatial": qkv_spatial, "out_spatial": out_spatial, "qkv_temporal": qkv_temporal, "out_temporal": out_temporal, "spatial_mask": spatial_mask, "temporal_mask": temporal_mask, "cotangent": cotangent}


def normalize(row_block):
    values = row_block.astype(jnp.float32)
    center = values - lax.optimization_barrier(jnp.mean(values, axis=-1, keepdims=True))
    inverse = lax.rsqrt(lax.optimization_barrier(jnp.mean(center * center, axis=-1, keepdims=True)) + 1e-06)
    return (center * inverse, inverse)

def round_narrow(values):
    return lax.optimization_barrier(values.astype(jnp.bfloat16)).astype(jnp.float32)

def expand_blocks(block_mask):
    grid_mask = jnp.broadcast_to(block_mask[:, None, :, None], (NB, BLK, NB, BLK)).reshape(P_SIZE, P_SIZE) == 1
    block_ids = jnp.arange(P_SIZE) // BLK
    return grid_mask | (block_ids[:, None] == block_ids[None, :])

def frame_rule(frame_mask):
    frame_ids = jnp.arange(FRAMES)
    return (frame_ids[:, None] >= frame_ids[None, :]) & ((frame_mask == 1) | (frame_ids[:, None] == frame_ids[None, :]))

def attention_probs(query_rows, key_matrix, allowed):
    logit_scores = jnp.einsum('vct,act->cva', query_rows.astype(jnp.float32), key_matrix.astype(jnp.float32)) * HEAD_SIZE ** (-0.5)
    logit_scores = jnp.where(allowed[None], logit_scores, -1e+30)
    weights = jnp.exp(logit_scores - lax.optimization_barrier(jnp.max(logit_scores, axis=-1, keepdims=True)))
    return weights / lax.optimization_barrier(jnp.sum(weights, axis=-1, keepdims=True))

def attend_forward(query_rows, key_matrix, value_matrix, allowed):
    softmax_weights = attention_probs(query_rows, key_matrix, allowed)
    blended_rows = jnp.einsum('nog,gnr->onr', round_narrow(softmax_weights), value_matrix.astype(jnp.float32))
    return blended_rows.astype(jnp.bfloat16)

def attend_backward(query_rows, key_matrix, value_matrix, allowed, grad_mixed):
    softmax_weights = attention_probs(query_rows, key_matrix, allowed)
    gradient_wide = grad_mixed.astype(jnp.float32)
    value_gradient = jnp.einsum('coz,ock->zck', round_narrow(softmax_weights), gradient_wide).astype(jnp.bfloat16)
    probability_gradient = jnp.einsum('vct,act->cva', gradient_wide, value_matrix.astype(jnp.float32))
    row_delta = lax.optimization_barrier(jnp.sum(softmax_weights * probability_gradient, axis=-1, keepdims=True))
    score_gradient = round_narrow(softmax_weights * (probability_gradient - row_delta) * HEAD_SIZE ** (-0.5))
    query_gradient = jnp.einsum('nog,gnr->onr', score_gradient, key_matrix.astype(jnp.float32)).astype(jnp.bfloat16)
    key_gradient = jnp.einsum('coz,ock->zck', score_gradient, query_rows.astype(jnp.float32)).astype(jnp.bfloat16)
    return jnp.stack([query_gradient, key_gradient, value_gradient])

def forward_layer(row_block, qkv_weights, out_weights, mask_table, allow_rule):
    batch_count, length, feature_count = row_block.shape
    normed, inverse = normalize(row_block)
    flat_rows = normed.astype(jnp.bfloat16).reshape(batch_count * length, feature_count)
    projected = jnp.stack([jnp.dot(flat_rows, qkv_weights[0], preferred_element_type=jnp.float32), jnp.dot(flat_rows, qkv_weights[1], preferred_element_type=jnp.float32), jnp.dot(flat_rows, qkv_weights[2], preferred_element_type=jnp.float32)]).astype(jnp.bfloat16)
    shaped = projected.reshape(3, batch_count, length, HEADS, HEAD_SIZE)

    def one_item(packed):
        query_rows, key_matrix, value_matrix, item_mask = packed
        return attend_forward(query_rows, key_matrix, value_matrix, allow_rule(item_mask))
    blended_rows = lax.map(one_item, (shaped[0], shaped[1], shaped[2], mask_table))
    blended_rows = blended_rows.reshape(batch_count * length, feature_count)
    update = jnp.dot(blended_rows, out_weights, preferred_element_type=jnp.float32)
    output = (row_block.astype(jnp.float32) + update.reshape(row_block.shape)).astype(jnp.bfloat16)
    return (output, (normed, inverse, flat_rows, shaped, blended_rows))

def backward_layer(grad_rows, qkv_weights, out_weights, mask_table, allow_rule, saved_state):
    normed, inverse, flat_rows, shaped, blended_rows = saved_state
    batch_count, length, feature_count = grad_rows.shape
    grad_flat = grad_rows.reshape(batch_count * length, feature_count)
    out_grad = jnp.dot(blended_rows.T, grad_flat, preferred_element_type=jnp.float32)
    grad_mixed = jnp.dot(grad_flat, out_weights.T, preferred_element_type=jnp.float32).astype(jnp.bfloat16)
    grad_mixed = grad_mixed.reshape(batch_count, length, HEADS, HEAD_SIZE)

    def one_item(packed):
        query_rows, key_matrix, value_matrix, item_mask, grad_item = packed
        return attend_backward(query_rows, key_matrix, value_matrix, allow_rule(item_mask), grad_item)
    qkv_grads = lax.map(one_item, (shaped[0], shaped[1], shaped[2], mask_table, grad_mixed))
    qkv_grads = jnp.moveaxis(qkv_grads, 1, 0).reshape(3, batch_count * length, feature_count)
    qkv_grad = jnp.stack([jnp.dot(flat_rows.T, qkv_grads[0], preferred_element_type=jnp.float32), jnp.dot(flat_rows.T, qkv_grads[1], preferred_element_type=jnp.float32), jnp.dot(flat_rows.T, qkv_grads[2], preferred_element_type=jnp.float32)])
    grad_normed = jnp.dot(qkv_grads[0], qkv_weights[0].T, preferred_element_type=jnp.float32)
    grad_normed = grad_normed + jnp.dot(qkv_grads[1], qkv_weights[1].T, preferred_element_type=jnp.float32)
    grad_normed = grad_normed + jnp.dot(qkv_grads[2], qkv_weights[2].T, preferred_element_type=jnp.float32)
    grad_normed = grad_normed.reshape(grad_rows.shape)
    mean_first = lax.optimization_barrier(jnp.mean(grad_normed, axis=-1, keepdims=True))
    mean_second = lax.optimization_barrier(jnp.mean(grad_normed * normed, axis=-1, keepdims=True))
    grad_in = grad_rows.astype(jnp.float32) + inverse * (grad_normed - mean_first - normed * mean_second)
    return (grad_in.astype(jnp.bfloat16), qkv_grad, out_grad)

def reference(frames, qkv_spatial, out_spatial, qkv_temporal, out_temporal, spatial_mask, temporal_mask, cotangent):
    hidden, spatial_state = forward_layer(frames, qkv_spatial, out_spatial, spatial_mask, expand_blocks)
    position_masks = jnp.repeat(temporal_mask, BLK, axis=0)
    by_position = jnp.transpose(hidden, (1, 0, 2))
    temporal_out, temporal_state = forward_layer(by_position, qkv_temporal, out_temporal, position_masks, frame_rule)
    result = jnp.transpose(temporal_out, (1, 0, 2))
    grad_position, temporal_qkv_grad, temporal_out_grad = backward_layer(jnp.transpose(cotangent, (1, 0, 2)), qkv_temporal, out_temporal, position_masks, frame_rule, temporal_state)
    hidden_grad = jnp.transpose(grad_position, (1, 0, 2))
    frames_grad, spatial_qkv_grad, spatial_out_grad = backward_layer(hidden_grad, qkv_spatial, out_spatial, spatial_mask, expand_blocks, spatial_state)
    return (result, frames_grad, spatial_qkv_grad, spatial_out_grad, temporal_qkv_grad, temporal_out_grad)
```

```python
import jax
import jax.numpy as jnp
from jax import lax
from jax.sharding import PartitionSpec as P

HEAD_SIZE = 72


def row_features(share_rows):
    return lax.all_gather(share_rows, "heads", axis=1, tiled=True)


def relayout(block_rows):
    return lax.all_to_all(block_rows, "seq", split_axis=1, concat_axis=0, tiled=True)


def normalize(full_rows):
    values = full_rows.astype(jnp.float32)
    mean = jnp.mean(values, axis=-1, keepdims=True)
    center = values - mean
    inverse = lax.rsqrt(jnp.mean(center * center, axis=-1, keepdims=True) + 1e-06)
    return (center * inverse, mean, inverse)


def attention_probs(query_rows, key_matrix, allowed):
    logit_scores = jnp.einsum(
        "lbhd,mbhd->bhlm", query_rows, key_matrix, preferred_element_type=jnp.float32
    ) * HEAD_SIZE ** (-0.5)
    logit_scores = jnp.where(allowed[:, None], logit_scores, -1e30)
    weights = jnp.exp(logit_scores - jnp.max(logit_scores, axis=-1, keepdims=True))
    return weights / jnp.sum(weights, axis=-1, keepdims=True)


def attend_forward(query_rows, key_matrix, value_matrix, allowed):
    softmax_weights = attention_probs(query_rows, key_matrix, allowed)
    blended_rows = jnp.einsum(
        "bhlm,mbhd->lbhd",
        softmax_weights.astype(jnp.bfloat16),
        value_matrix,
        preferred_element_type=jnp.float32,
    )
    return blended_rows.astype(jnp.bfloat16)


def attend_backward(query_rows, key_matrix, value_matrix, allowed, grad_mixed):
    softmax_weights = attention_probs(query_rows, key_matrix, allowed)
    value_gradient = jnp.einsum(
        "bhlm,lbhd->mbhd",
        softmax_weights.astype(jnp.bfloat16),
        grad_mixed,
        preferred_element_type=jnp.float32,
    ).astype(jnp.bfloat16)
    probability_gradient = jnp.einsum(
        "lbhd,mbhd->bhlm", grad_mixed, value_matrix, preferred_element_type=jnp.float32
    )
    row_delta = jnp.sum(softmax_weights * probability_gradient, axis=-1, keepdims=True)
    score_gradient = (
        softmax_weights * (probability_gradient - row_delta) * HEAD_SIZE ** (-0.5)
    ).astype(jnp.bfloat16)
    query_gradient = jnp.einsum(
        "bhlm,mbhd->lbhd", score_gradient, key_matrix, preferred_element_type=jnp.float32
    ).astype(jnp.bfloat16)
    key_gradient = jnp.einsum(
        "bhlm,lbhd->mbhd", score_gradient, query_rows, preferred_element_type=jnp.float32
    ).astype(jnp.bfloat16)
    return (query_gradient, key_gradient, value_gradient)


def layer_forward(share_rows, full_rows, qkv_weights, out_weights, allowed, length, batch_count):
    own_width = share_rows.shape[1]
    normed, mean, inverse = normalize(full_rows)
    normed_low = normed.astype(jnp.bfloat16)
    projected = jnp.einsum(
        "nd,kde->kne", normed_low, qkv_weights, preferred_element_type=jnp.float32
    ).astype(jnp.bfloat16)
    shaped = projected.reshape(3, length, batch_count, own_width // HEAD_SIZE, HEAD_SIZE)
    blended_rows = attend_forward(shaped[0], shaped[1], shaped[2], allowed).reshape(
        length * batch_count, own_width
    )
    update = jnp.dot(blended_rows, out_weights, preferred_element_type=jnp.float32)
    return (update.astype(jnp.bfloat16), (normed, mean, inverse, normed_low, shaped, blended_rows))


def add_update(share_rows, update):
    summed = lax.psum_scatter(update, "heads", scatter_dimension=1, tiled=True)
    return (share_rows.astype(jnp.float32) + summed.astype(jnp.float32)).astype(jnp.bfloat16)


def layer_backward(share_rows, grad_share, grad_rows, qkv_weights, out_weights, allowed, saved):
    normed, mean, inverse, normed_low, shaped, blended_rows = saved
    rows, own_width = grad_share.shape
    groups = lax.axis_size("heads")
    out_grad = jnp.einsum("nd,nk->dk", grad_rows, blended_rows, preferred_element_type=jnp.float32)
    grad_mixed = jnp.einsum(
        "nd,kd->nk", grad_rows, out_weights, preferred_element_type=jnp.float32
    ).astype(jnp.bfloat16)
    grad_mixed = grad_mixed.reshape(shaped.shape[1:])
    query_gradient, key_gradient, value_gradient = attend_backward(
        shaped[0], shaped[1], shaped[2], allowed, grad_mixed
    )
    qkv_grads = jnp.stack([query_gradient, key_gradient, value_gradient]).reshape(3, -1, own_width)
    qkv_grad = jnp.einsum("nd,kne->dke", normed_low, qkv_grads, preferred_element_type=jnp.float32)
    weight_grads = jnp.concatenate([qkv_grad, out_grad[:, None]], axis=1).astype(jnp.bfloat16)
    weight_grads = weight_grads.reshape(-1, 4 * own_width)
    partial_term = jnp.einsum(
        "kne,kde->dn", qkv_grads, qkv_weights, preferred_element_type=jnp.float32
    )
    features = partial_term.shape[0]
    first = jnp.sum(partial_term, axis=0) / features
    second = jnp.sum(partial_term * normed.T, axis=0) / features
    extra = jnp.concatenate([first[None], second[None], jnp.zeros((14, rows), jnp.float32)])
    packed = jnp.concatenate(
        [
            partial_term.reshape(groups, own_width, rows).astype(jnp.bfloat16),
            jnp.broadcast_to(extra.astype(jnp.bfloat16)[None], (groups, 16, rows)),
        ],
        axis=1,
    ).reshape(groups * (own_width + 16), rows)
    summed = lax.psum_scatter(packed, "heads", scatter_dimension=0, tiled=True)
    summed = summed.astype(jnp.float32)
    whole = summed[:own_width].T
    mean_first = summed[own_width][:, None]
    mean_second = summed[own_width + 1][:, None]
    own_normed = (share_rows.astype(jnp.float32) - mean) * inverse
    own_grad = inverse * (whole - mean_first - own_normed * mean_second)
    grad_in = (grad_share.astype(jnp.float32) + own_grad).astype(jnp.bfloat16)
    return (grad_in, weight_grads)


def sum_weight_grads(weight_grads, own_width):
    summed = lax.psum_scatter(weight_grads, "seq", scatter_dimension=0, tiled=True)
    summed = summed.astype(jnp.float32).reshape(-1, 4, own_width)
    return (jnp.swapaxes(summed[:, :3], 0, 1), summed[:, 3].T)


def shards(
    frames,
    qkv_spatial,
    out_spatial,
    qkv_temporal,
    out_temporal,
    spatial_mask,
    temporal_mask,
    cotangent,
):
    length = frames.shape[1]
    own_width = frames.shape[2]
    frame_count = temporal_mask.shape[1]
    local_count = length // lax.axis_size("seq")
    block_count = spatial_mask.shape[1]
    block_size = length // block_count
    grid_mask = (
        jnp.broadcast_to(
            spatial_mask[0][:, None, :, None], (block_count, block_size, block_count, block_size)
        ).reshape(length, length)
        == 1
    )
    block_ids = jnp.arange(length) // block_size
    spatial_allowed = (grid_mask | (block_ids[:, None] == block_ids[None, :]))[None]
    positions = lax.axis_index("seq") * local_count + jnp.arange(local_count)
    chosen = (positions // block_size)[:, None] == jnp.arange(block_count)[None, :]
    picked = jnp.sum(jnp.where(chosen[:, :, None, None], temporal_mask[None], 0), axis=1)
    frame_ids = jnp.arange(frame_count)
    causal = (frame_ids[:, None] >= frame_ids[None, :])[None]
    diagonal = (frame_ids[:, None] == frame_ids[None, :])[None]
    temporal_allowed = causal & ((picked == 1) | diagonal)
    frame_share = frames.reshape(length, own_width)
    cotangent_share = cotangent.reshape(length, own_width)
    frame_rows = row_features(frame_share)
    cotangent_share, frame_rows = lax.optimization_barrier((cotangent_share, frame_rows))
    cotangent_rows = row_features(cotangent_share)
    update, spatial_state = layer_forward(
        frame_share, frame_rows, qkv_spatial, out_spatial, spatial_allowed, length, 1
    )
    hidden = add_update(frame_share, update)
    position_share = relayout(hidden.reshape(1, length, own_width)).reshape(length, own_width)
    position_rows = row_features(position_share)
    late_update, temporal_state = layer_forward(
        position_share,
        position_rows,
        qkv_temporal,
        out_temporal,
        temporal_allowed,
        frame_count,
        local_count,
    )
    grad_position, temporal_grads = layer_backward(
        position_share,
        cotangent_share,
        cotangent_rows,
        qkv_temporal,
        out_temporal,
        temporal_allowed,
        temporal_state,
    )
    hidden_grad = relayout(grad_position.reshape(1, length, own_width)).reshape(length, own_width)
    hidden_grad_rows = row_features(hidden_grad)
    late_update, hidden_grad_rows = lax.optimization_barrier((late_update, hidden_grad_rows))
    result = add_update(position_share, late_update)
    frames_grad, spatial_grads = layer_backward(
        frame_share,
        hidden_grad,
        hidden_grad_rows,
        qkv_spatial,
        out_spatial,
        spatial_allowed,
        spatial_state,
    )
    reduced = sum_weight_grads(spatial_grads, own_width) + sum_weight_grads(
        temporal_grads, own_width
    )
    return (
        result.reshape(frame_count, local_count, own_width),
        frames_grad.reshape(1, length, own_width),
        reduced[0],
        reduced[1],
        reduced[2],
        reduced[3],
    )


def solution(mesh):
    placed = (
        P("seq", None, "heads"),
        P(None, None, "heads"),
        P("heads", None),
        P(None, None, "heads"),
        P("heads", None),
        P("seq", None, None),
        P(),
        P(None, "seq", "heads"),
    )
    return jax.shard_map(
        shards,
        mesh=mesh,
        in_specs=placed,
        out_specs=(
            P(None, "seq", "heads"),
            P("seq", None, "heads"),
            P(None, "seq", "heads"),
            P("heads", "seq"),
            P(None, "seq", "heads"),
            P("heads", "seq"),
        ),
        check_vma=False,
    )
```

```python
import jax
import jax.numpy as jnp
from jax import lax
from jax.sharding import PartitionSpec as P

HEAD_SIZE = 72


def row_features(share_rows):
    return lax.all_gather(share_rows, "heads", axis=1, tiled=True)


def relayout(block_rows):
    return lax.all_to_all(block_rows, "seq", split_axis=1, concat_axis=0, tiled=True)


def normalize(full_rows):
    values = full_rows.astype(jnp.float32)
    mean = jnp.mean(values, axis=-1, keepdims=True)
    center = values - mean
    inverse = lax.rsqrt(jnp.mean(center * center, axis=-1, keepdims=True) + 1e-06)
    return (center * inverse, mean, inverse)


def attention_probs(query_rows, key_matrix, allowed):
    logit_scores = jnp.einsum(
        "lbhd,mbhd->bhlm", query_rows, key_matrix, preferred_element_type=jnp.float32
    ) * HEAD_SIZE ** (-0.5)
    logit_scores = jnp.where(allowed[:, None], logit_scores, -1e30)
    weights = jnp.exp(logit_scores - jnp.max(logit_scores, axis=-1, keepdims=True))
    return weights / jnp.sum(weights, axis=-1, keepdims=True)


def attend_forward(query_rows, key_matrix, value_matrix, allowed):
    softmax_weights = attention_probs(query_rows, key_matrix, allowed)
    blended_rows = jnp.einsum(
        "bhlm,mbhd->lbhd",
        softmax_weights.astype(jnp.bfloat16),
        value_matrix,
        preferred_element_type=jnp.float32,
    )
    return blended_rows.astype(jnp.bfloat16)


def attend_backward(query_rows, key_matrix, value_matrix, allowed, grad_mixed):
    softmax_weights = attention_probs(query_rows, key_matrix, allowed)
    value_gradient = jnp.einsum(
        "bhlm,lbhd->mbhd",
        softmax_weights.astype(jnp.bfloat16),
        grad_mixed,
        preferred_element_type=jnp.float32,
    ).astype(jnp.bfloat16)
    probability_gradient = jnp.einsum(
        "lbhd,mbhd->bhlm", grad_mixed, value_matrix, preferred_element_type=jnp.float32
    )
    row_delta = jnp.sum(softmax_weights * probability_gradient, axis=-1, keepdims=True)
    score_gradient = (
        softmax_weights * (probability_gradient - row_delta) * HEAD_SIZE ** (-0.5)
    ).astype(jnp.bfloat16)
    query_gradient = jnp.einsum(
        "bhlm,mbhd->lbhd", score_gradient, key_matrix, preferred_element_type=jnp.float32
    ).astype(jnp.bfloat16)
    key_gradient = jnp.einsum(
        "bhlm,lbhd->mbhd", score_gradient, query_rows, preferred_element_type=jnp.float32
    ).astype(jnp.bfloat16)
    return (query_gradient, key_gradient, value_gradient)


def layer_forward(share_rows, full_rows, qkv_weights, out_weights, allowed, length, batch_count):
    own_width = share_rows.shape[1]
    normed, mean, inverse = normalize(full_rows)
    normed_low = normed.astype(jnp.bfloat16)
    projected = jnp.einsum(
        "nd,kde->kne", normed_low, qkv_weights, preferred_element_type=jnp.float32
    ).astype(jnp.bfloat16)
    shaped = projected.reshape(3, length, batch_count, own_width // HEAD_SIZE, HEAD_SIZE)
    blended_rows = attend_forward(shaped[0], shaped[1], shaped[2], allowed).reshape(
        length * batch_count, own_width
    )
    update = jnp.dot(blended_rows, out_weights, preferred_element_type=jnp.float32)
    return (update.astype(jnp.bfloat16), (normed, mean, inverse, normed_low, shaped, blended_rows))


def add_update(share_rows, update):
    summed = lax.psum_scatter(update, "heads", scatter_dimension=1, tiled=True)
    return (share_rows.astype(jnp.float32) + summed.astype(jnp.float32)).astype(jnp.bfloat16)


def layer_backward(
    share_rows, grad_share, grad_rows, qkv_weights, out_weights, allowed, saved, before=()
):
    normed, mean, inverse, normed_low, shaped, blended_rows = saved
    rows, own_width = grad_share.shape
    groups = lax.axis_size("heads")
    out_grad = jnp.einsum("nd,nk->dk", grad_rows, blended_rows, preferred_element_type=jnp.float32)
    grad_mixed = jnp.einsum(
        "nd,kd->nk", grad_rows, out_weights, preferred_element_type=jnp.float32
    ).astype(jnp.bfloat16)
    grad_mixed = grad_mixed.reshape(shaped.shape[1:])
    query_gradient, key_gradient, value_gradient = attend_backward(
        shaped[0], shaped[1], shaped[2], allowed, grad_mixed
    )
    qkv_grads = jnp.stack([query_gradient, key_gradient, value_gradient]).reshape(3, -1, own_width)
    qkv_grad = jnp.einsum("nd,kne->dke", normed_low, qkv_grads, preferred_element_type=jnp.float32)
    weight_grads = jnp.concatenate([qkv_grad, out_grad[:, None]], axis=1).astype(jnp.bfloat16)
    weight_grads = weight_grads.reshape(-1, 4 * own_width)
    partial_term = jnp.einsum(
        "kne,kde->dn", qkv_grads, qkv_weights, preferred_element_type=jnp.float32
    )
    features = partial_term.shape[0]
    first = jnp.sum(partial_term, axis=0) / features
    second = jnp.sum(partial_term * normed.T, axis=0) / features
    extra = jnp.concatenate([first[None], second[None], jnp.zeros((14, rows), jnp.float32)])
    packed = jnp.concatenate(
        [
            partial_term.reshape(groups, own_width, rows).astype(jnp.bfloat16),
            jnp.broadcast_to(extra.astype(jnp.bfloat16)[None], (groups, 16, rows)),
        ],
        axis=1,
    ).reshape(groups * (own_width + 16), rows)
    packed, before = lax.optimization_barrier((packed, before))
    summed = lax.psum_scatter(packed, "heads", scatter_dimension=0, tiled=True)
    summed = summed.astype(jnp.float32)
    whole = summed[:own_width].T
    mean_first = summed[own_width][:, None]
    mean_second = summed[own_width + 1][:, None]
    own_normed = (share_rows.astype(jnp.float32) - mean) * inverse
    own_grad = inverse * (whole - mean_first - own_normed * mean_second)
    grad_in = (grad_share.astype(jnp.float32) + own_grad).astype(jnp.bfloat16)
    return (grad_in, weight_grads, before)


def exchange_grads(weight_grads):
    members = lax.axis_size("seq")
    blocks = weight_grads.reshape(members, -1, weight_grads.shape[1])
    shares = lax.all_to_all(blocks, "seq", split_axis=0, concat_axis=0, tiled=True)
    return jnp.sum(shares.astype(jnp.float32), axis=0)


def split_grads(summed, own_width):
    summed = summed.reshape(-1, 4, own_width)
    return (jnp.swapaxes(summed[:, :3], 0, 1), summed[:, 3].T)


def shards(
    frames,
    qkv_spatial,
    out_spatial,
    qkv_temporal,
    out_temporal,
    spatial_mask,
    temporal_mask,
    cotangent,
):
    length = frames.shape[1]
    own_width = frames.shape[2]
    frame_count = temporal_mask.shape[1]
    local_count = length // lax.axis_size("seq")
    block_count = spatial_mask.shape[1]
    block_size = length // block_count
    grid_mask = (
        jnp.broadcast_to(
            spatial_mask[0][:, None, :, None], (block_count, block_size, block_count, block_size)
        ).reshape(length, length)
        == 1
    )
    block_ids = jnp.arange(length) // block_size
    spatial_allowed = (grid_mask | (block_ids[:, None] == block_ids[None, :]))[None]
    positions = lax.axis_index("seq") * local_count + jnp.arange(local_count)
    chosen = (positions // block_size)[:, None] == jnp.arange(block_count)[None, :]
    picked = jnp.sum(jnp.where(chosen[:, :, None, None], temporal_mask[None], 0), axis=1)
    frame_ids = jnp.arange(frame_count)
    causal = (frame_ids[:, None] >= frame_ids[None, :])[None]
    diagonal = (frame_ids[:, None] == frame_ids[None, :])[None]
    temporal_allowed = causal & ((picked == 1) | diagonal)
    frame_share = frames.reshape(length, own_width)
    cotangent_share = cotangent.reshape(length, own_width)
    frame_rows = row_features(frame_share)
    cotangent_share, frame_rows = lax.optimization_barrier((cotangent_share, frame_rows))
    half = length // 2
    early_rows = row_features(cotangent_share[:half])
    update, spatial_state = layer_forward(
        frame_share, frame_rows, qkv_spatial, out_spatial, spatial_allowed, length, 1
    )
    update, early_rows = lax.optimization_barrier((update, early_rows))
    hidden = add_update(frame_share, update)
    late_cotangent, hidden = lax.optimization_barrier((cotangent_share[half:], hidden))
    late_rows = row_features(late_cotangent)
    cotangent_rows = jnp.concatenate([early_rows, late_rows])
    position_share = relayout(hidden.reshape(1, length, own_width)).reshape(length, own_width)
    position_rows = row_features(position_share)
    late_update, temporal_state = layer_forward(
        position_share,
        position_rows,
        qkv_temporal,
        out_temporal,
        temporal_allowed,
        frame_count,
        local_count,
    )
    grad_position, temporal_grads, _ = layer_backward(
        position_share,
        cotangent_share,
        cotangent_rows,
        qkv_temporal,
        out_temporal,
        temporal_allowed,
        temporal_state,
    )
    hidden_grad = relayout(grad_position.reshape(1, length, own_width)).reshape(length, own_width)
    hidden_grad_rows = row_features(hidden_grad)
    late_update, temporal_grads, hidden_grad_rows = lax.optimization_barrier(
        (late_update, temporal_grads, hidden_grad_rows)
    )
    result = add_update(position_share, late_update)
    temporal_sums = lax.psum_scatter(temporal_grads, "seq", scatter_dimension=0, tiled=True)
    frames_grad, spatial_grads, early = layer_backward(
        frame_share,
        hidden_grad,
        hidden_grad_rows,
        qkv_spatial,
        out_spatial,
        spatial_allowed,
        spatial_state,
        (result, temporal_sums),
    )
    result, temporal_sums = early
    reduced = split_grads(exchange_grads(spatial_grads), own_width) + split_grads(
        temporal_sums.astype(jnp.float32), own_width
    )
    return (
        result.reshape(frame_count, local_count, own_width),
        frames_grad.reshape(1, length, own_width),
        reduced[0],
        reduced[1],
        reduced[2],
        reduced[3],
    )


def solution(mesh):
    placed = (
        P("seq", None, "heads"),
        P(None, None, "heads"),
        P("heads", None),
        P(None, None, "heads"),
        P("heads", None),
        P("seq", None, None),
        P(),
        P(None, "seq", "heads"),
    )
    return jax.shard_map(
        shards,
        mesh=mesh,
        in_specs=placed,
        out_specs=(
            P(None, "seq", "heads"),
            P("seq", None, "heads"),
            P(None, "seq", "heads"),
            P("heads", "seq"),
            P(None, "seq", "heads"),
            P("heads", "seq"),
        ),
        check_vma=False,
    )
```

```python
import jax
import jax.numpy as jnp
from jax import lax
from jax.sharding import PartitionSpec as P

HEAD_SIZE = 72


def row_features(share_rows):
    return lax.all_gather(share_rows, "heads", axis=1, tiled=True)


def relayout(block_rows):
    return lax.all_to_all(block_rows, "seq", split_axis=1, concat_axis=0, tiled=True)


def normalize(full_rows):
    values = full_rows.astype(jnp.float32)
    mean = jnp.mean(values, axis=-1, keepdims=True)
    center = values - mean
    inverse = lax.rsqrt(jnp.mean(center * center, axis=-1, keepdims=True) + 1e-06)
    return (center * inverse, mean, inverse)


def attention_probs(query_rows, key_matrix, allowed):
    logit_scores = jnp.einsum(
        "lbhd,mbhd->bhlm", query_rows, key_matrix, preferred_element_type=jnp.float32
    ) * HEAD_SIZE ** (-0.5)
    logit_scores = jnp.where(allowed[:, None], logit_scores, -1e30)
    weights = jnp.exp(logit_scores - jnp.max(logit_scores, axis=-1, keepdims=True))
    return weights / jnp.sum(weights, axis=-1, keepdims=True)


def attend_forward(query_rows, key_matrix, value_matrix, allowed):
    softmax_weights = attention_probs(query_rows, key_matrix, allowed)
    blended_rows = jnp.einsum(
        "bhlm,mbhd->lbhd",
        softmax_weights.astype(jnp.bfloat16),
        value_matrix,
        preferred_element_type=jnp.float32,
    )
    return blended_rows.astype(jnp.bfloat16)


def attend_backward(query_rows, key_matrix, value_matrix, allowed, grad_mixed):
    softmax_weights = attention_probs(query_rows, key_matrix, allowed)
    value_gradient = jnp.einsum(
        "bhlm,lbhd->mbhd",
        softmax_weights.astype(jnp.bfloat16),
        grad_mixed,
        preferred_element_type=jnp.float32,
    ).astype(jnp.bfloat16)
    probability_gradient = jnp.einsum(
        "lbhd,mbhd->bhlm", grad_mixed, value_matrix, preferred_element_type=jnp.float32
    )
    row_delta = jnp.sum(softmax_weights * probability_gradient, axis=-1, keepdims=True)
    score_gradient = (
        softmax_weights * (probability_gradient - row_delta) * HEAD_SIZE ** (-0.5)
    ).astype(jnp.bfloat16)
    if query_rows.shape[1] == 1:
        score_gradient = lax.optimization_barrier(score_gradient)
    query_gradient = jnp.einsum(
        "bhlm,mbhd->lbhd", score_gradient, key_matrix, preferred_element_type=jnp.float32
    ).astype(jnp.bfloat16)
    key_gradient = jnp.einsum(
        "bhlm,lbhd->mbhd", score_gradient, query_rows, preferred_element_type=jnp.float32
    ).astype(jnp.bfloat16)
    return (query_gradient, key_gradient, value_gradient)


def layer_forward(share_rows, full_rows, qkv_weights, out_weights, allowed, length, batch_count):
    own_width = share_rows.shape[1]
    normed, mean, inverse = normalize(full_rows)
    normed_low = normed.astype(jnp.bfloat16)
    projected = jnp.einsum(
        "nd,kde->kne", normed_low, qkv_weights, preferred_element_type=jnp.float32
    ).astype(jnp.bfloat16)
    shaped = projected.reshape(3, length, batch_count, own_width // HEAD_SIZE, HEAD_SIZE)
    blended_rows = attend_forward(shaped[0], shaped[1], shaped[2], allowed).reshape(
        length * batch_count, own_width
    )
    update = jnp.dot(blended_rows, out_weights, preferred_element_type=jnp.float32)
    return (update.astype(jnp.bfloat16), (normed, mean, inverse, normed_low, shaped, blended_rows))


def add_update(share_rows, update):
    summed = lax.psum_scatter(update, "heads", scatter_dimension=1, tiled=True)
    return (share_rows.astype(jnp.float32) + summed.astype(jnp.float32)).astype(jnp.bfloat16)


def layer_backward(
    share_rows, grad_share, grad_rows, qkv_weights, out_weights, allowed, saved, before=()
):
    normed, mean, inverse, normed_low, shaped, blended_rows = saved
    rows, own_width = grad_share.shape
    groups = lax.axis_size("heads")
    out_grad = jnp.einsum("nd,nk->dk", grad_rows, blended_rows, preferred_element_type=jnp.float32)
    grad_mixed = jnp.einsum(
        "nd,kd->nk", grad_rows, out_weights, preferred_element_type=jnp.float32
    ).astype(jnp.bfloat16)
    grad_mixed = grad_mixed.reshape(shaped.shape[1:])
    query_gradient, key_gradient, value_gradient = attend_backward(
        shaped[0], shaped[1], shaped[2], allowed, grad_mixed
    )
    qkv_grads = jnp.stack([query_gradient, key_gradient, value_gradient]).reshape(3, -1, own_width)
    qkv_grad = jnp.einsum("nd,kne->dke", normed_low, qkv_grads, preferred_element_type=jnp.float32)
    weight_grads = jnp.concatenate([qkv_grad, out_grad[:, None]], axis=1).astype(jnp.bfloat16)
    weight_grads = weight_grads.reshape(-1, 4 * own_width)
    partial_term = jnp.einsum(
        "kne,kde->dn", qkv_grads, qkv_weights, preferred_element_type=jnp.float32
    )
    features = partial_term.shape[0]
    first = jnp.sum(partial_term, axis=0) / features
    second = jnp.sum(partial_term * normed.T, axis=0) / features
    extra = jnp.concatenate([first[None], second[None], jnp.zeros((14, rows), jnp.float32)])
    packed = jnp.concatenate(
        [
            partial_term.reshape(groups, own_width, rows).astype(jnp.bfloat16),
            jnp.broadcast_to(extra.astype(jnp.bfloat16)[None], (groups, 16, rows)),
        ],
        axis=1,
    ).reshape(groups * (own_width + 16), rows)
    packed, before = lax.optimization_barrier((packed, before))
    summed = lax.psum_scatter(packed, "heads", scatter_dimension=0, tiled=True)
    summed = summed.astype(jnp.float32)
    whole = summed[:own_width].T
    mean_first = summed[own_width][:, None]
    mean_second = summed[own_width + 1][:, None]
    own_normed = (share_rows.astype(jnp.float32) - mean) * inverse
    own_grad = inverse * (whole - mean_first - own_normed * mean_second)
    grad_in = (grad_share.astype(jnp.float32) + own_grad).astype(jnp.bfloat16)
    return (grad_in, weight_grads, before)


def exchange_grads(weight_grads):
    members = lax.axis_size("seq")
    blocks = weight_grads.reshape(members, -1, weight_grads.shape[1])
    shares = lax.all_to_all(blocks, "seq", split_axis=0, concat_axis=0, tiled=True)
    return jnp.sum(shares.astype(jnp.float32), axis=0)


def split_grads(summed, own_width):
    summed = summed.reshape(-1, 4, own_width)
    return (jnp.swapaxes(summed[:, :3], 0, 1), summed[:, 3].T)


def shards(
    frames,
    qkv_spatial,
    out_spatial,
    qkv_temporal,
    out_temporal,
    spatial_mask,
    temporal_mask,
    cotangent,
):
    length = frames.shape[1]
    own_width = frames.shape[2]
    frame_count = temporal_mask.shape[1]
    local_count = length // lax.axis_size("seq")
    block_count = spatial_mask.shape[1]
    block_size = length // block_count
    grid_mask = (
        jnp.broadcast_to(
            spatial_mask[0][:, None, :, None], (block_count, block_size, block_count, block_size)
        ).reshape(length, length)
        == 1
    )
    block_ids = jnp.arange(length) // block_size
    spatial_allowed = (grid_mask | (block_ids[:, None] == block_ids[None, :]))[None]
    positions = lax.axis_index("seq") * local_count + jnp.arange(local_count)
    chosen = (positions // block_size)[:, None] == jnp.arange(block_count)[None, :]
    picked = jnp.sum(jnp.where(chosen[:, :, None, None], temporal_mask[None], 0), axis=1)
    frame_ids = jnp.arange(frame_count)
    causal = (frame_ids[:, None] >= frame_ids[None, :])[None]
    diagonal = (frame_ids[:, None] == frame_ids[None, :])[None]
    temporal_allowed = causal & ((picked == 1) | diagonal)
    frame_share = frames.reshape(length, own_width)
    cotangent_share = cotangent.reshape(length, own_width)
    frame_rows = row_features(frame_share)
    cotangent_share, frame_rows = lax.optimization_barrier((cotangent_share, frame_rows))
    half = length // 2
    early_rows = row_features(cotangent_share[:half])
    update, spatial_state = layer_forward(
        frame_share, frame_rows, qkv_spatial, out_spatial, spatial_allowed, length, 1
    )
    update, early_rows = lax.optimization_barrier((update, early_rows))
    hidden = add_update(frame_share, update)
    late_cotangent, hidden = lax.optimization_barrier((cotangent_share[half:], hidden))
    late_rows = row_features(late_cotangent)
    cotangent_rows = jnp.concatenate([early_rows, late_rows])
    position_share = relayout(hidden.reshape(1, length, own_width)).reshape(length, own_width)
    position_rows = row_features(position_share)
    late_update, temporal_state = layer_forward(
        position_share,
        position_rows,
        qkv_temporal,
        out_temporal,
        temporal_allowed,
        frame_count,
        local_count,
    )
    grad_position, temporal_grads, _ = layer_backward(
        position_share,
        cotangent_share,
        cotangent_rows,
        qkv_temporal,
        out_temporal,
        temporal_allowed,
        temporal_state,
    )
    temporal_sums = exchange_grads(temporal_grads)
    grad_position, temporal_sums = lax.optimization_barrier((grad_position, temporal_sums))
    hidden_grad = relayout(grad_position.reshape(1, length, own_width)).reshape(length, own_width)
    hidden_grad_rows = row_features(hidden_grad)
    late_update, hidden_grad_rows = lax.optimization_barrier((late_update, hidden_grad_rows))
    result = add_update(position_share, late_update)
    frames_grad, spatial_grads, early = layer_backward(
        frame_share,
        hidden_grad,
        hidden_grad_rows,
        qkv_spatial,
        out_spatial,
        spatial_allowed,
        spatial_state,
        result,
    )
    result = early
    reduced = split_grads(exchange_grads(spatial_grads), own_width) + split_grads(
        temporal_sums, own_width
    )
    return (
        result.reshape(frame_count, local_count, own_width),
        frames_grad.reshape(1, length, own_width),
        reduced[0],
        reduced[1],
        reduced[2],
        reduced[3],
    )


def solution(mesh):
    placed = (
        P("seq", None, "heads"),
        P(None, None, "heads"),
        P("heads", None),
        P(None, None, "heads"),
        P("heads", None),
        P("seq", None, None),
        P(),
        P(None, "seq", "heads"),
    )
    return jax.shard_map(
        shards,
        mesh=mesh,
        in_specs=placed,
        out_specs=(
            P(None, "seq", "heads"),
            P("seq", None, "heads"),
            P(None, "seq", "heads"),
            P("heads", "seq"),
            P(None, "seq", "heads"),
            P("heads", "seq"),
        ),
        check_vma=False,
    )
```

```python
import jax
import jax.numpy as jnp
from jax import lax
from jax.sharding import PartitionSpec as P

HEAD_SIZE = 72


def row_features(share_rows):
    return lax.all_gather(share_rows, "heads", axis=1, tiled=True)


def relayout(block_rows):
    return lax.all_to_all(block_rows, "seq", split_axis=1, concat_axis=0, tiled=True)


def normalize(full_rows):
    values = full_rows.astype(jnp.float32)
    mean = jnp.mean(values, axis=-1, keepdims=True)
    center = values - mean
    inverse = lax.rsqrt(jnp.mean(center * center, axis=-1, keepdims=True) + 1e-06)
    return (center * inverse, mean, inverse)


def attention_probs(query_rows, key_matrix, allowed):
    logit_scores = jnp.einsum(
        "lbhd,mbhd->bhlm", query_rows, key_matrix, preferred_element_type=jnp.float32
    ) * HEAD_SIZE ** (-0.5)
    logit_scores = jnp.where(allowed[:, None], logit_scores, -1e30)
    weights = jnp.exp(logit_scores - jnp.max(logit_scores, axis=-1, keepdims=True))
    return weights / jnp.sum(weights, axis=-1, keepdims=True)


def attend_forward(query_rows, key_matrix, value_matrix, allowed):
    softmax_weights = attention_probs(query_rows, key_matrix, allowed)
    blended_rows = jnp.einsum(
        "bhlm,mbhd->lbhd",
        softmax_weights.astype(jnp.bfloat16),
        value_matrix,
        preferred_element_type=jnp.float32,
    )
    return blended_rows.astype(jnp.bfloat16)


def attend_backward(query_rows, key_matrix, value_matrix, allowed, grad_mixed):
    softmax_weights = attention_probs(query_rows, key_matrix, allowed)
    value_gradient = jnp.einsum(
        "bhlm,lbhd->mbhd",
        softmax_weights.astype(jnp.bfloat16),
        grad_mixed,
        preferred_element_type=jnp.float32,
    ).astype(jnp.bfloat16)
    probability_gradient = jnp.einsum(
        "lbhd,mbhd->bhlm", grad_mixed, value_matrix, preferred_element_type=jnp.float32
    )
    row_delta = jnp.sum(softmax_weights * probability_gradient, axis=-1, keepdims=True)
    score_gradient = (
        softmax_weights * (probability_gradient - row_delta) * HEAD_SIZE ** (-0.5)
    ).astype(jnp.bfloat16)
    if query_rows.shape[1] == 1:
        score_gradient = lax.optimization_barrier(score_gradient)
    query_gradient = jnp.einsum(
        "bhlm,mbhd->lbhd", score_gradient, key_matrix, preferred_element_type=jnp.float32
    ).astype(jnp.bfloat16)
    key_gradient = jnp.einsum(
        "bhlm,lbhd->mbhd", score_gradient, query_rows, preferred_element_type=jnp.float32
    ).astype(jnp.bfloat16)
    return (query_gradient, key_gradient, value_gradient)


def layer_forward(share_rows, full_rows, qkv_weights, out_weights, allowed, length, batch_count):
    own_width = share_rows.shape[1]
    normed, mean, inverse = normalize(full_rows)
    normed_low = normed.astype(jnp.bfloat16)
    projected = jnp.einsum(
        "nd,kde->kne", normed_low, qkv_weights, preferred_element_type=jnp.float32
    ).astype(jnp.bfloat16)
    shaped = projected.reshape(3, length, batch_count, own_width // HEAD_SIZE, HEAD_SIZE)
    blended_rows = attend_forward(shaped[0], shaped[1], shaped[2], allowed).reshape(
        length * batch_count, own_width
    )
    update = jnp.dot(blended_rows, out_weights, preferred_element_type=jnp.float32)
    return (update.astype(jnp.bfloat16), (normed, mean, inverse, normed_low, shaped, blended_rows))


def add_update(share_rows, update):
    summed = lax.psum_scatter(update, "heads", scatter_dimension=1, tiled=True)
    return (share_rows.astype(jnp.float32) + summed.astype(jnp.float32)).astype(jnp.bfloat16)


def layer_backward(
    share_rows, grad_share, grad_rows, qkv_weights, out_weights, allowed, saved, before=()
):
    normed, mean, inverse, normed_low, shaped, blended_rows = saved
    rows, own_width = grad_share.shape
    groups = lax.axis_size("heads")
    out_grad = jnp.einsum("nd,nk->dk", grad_rows, blended_rows, preferred_element_type=jnp.float32)
    grad_mixed = jnp.einsum(
        "nd,kd->nk", grad_rows, out_weights, preferred_element_type=jnp.float32
    ).astype(jnp.bfloat16)
    grad_mixed = grad_mixed.reshape(shaped.shape[1:])
    query_gradient, key_gradient, value_gradient = attend_backward(
        shaped[0], shaped[1], shaped[2], allowed, grad_mixed
    )
    qkv_grads = jnp.stack([query_gradient, key_gradient, value_gradient]).reshape(3, -1, own_width)
    qkv_grad = [
        jnp.einsum("nd,ne->de", normed_low, part, preferred_element_type=jnp.float32)
        for part in qkv_grads
    ]
    parts = qkv_grad + [out_grad]
    weight_grads = jnp.concatenate([part.astype(jnp.bfloat16) for part in parts], axis=1)
    partial_term = jnp.einsum(
        "kne,kde->dn", qkv_grads, qkv_weights, preferred_element_type=jnp.float32
    )
    features = partial_term.shape[0]
    first = jnp.sum(partial_term, axis=0) / features
    second = jnp.sum(partial_term * normed.T, axis=0) / features
    extra = jnp.concatenate([first[None], second[None], jnp.zeros((14, rows), jnp.float32)])
    packed = jnp.concatenate(
        [
            partial_term.reshape(groups, own_width, rows).astype(jnp.bfloat16),
            jnp.broadcast_to(extra.astype(jnp.bfloat16)[None], (groups, 16, rows)),
        ],
        axis=1,
    ).reshape(groups * (own_width + 16), rows)
    packed, before = lax.optimization_barrier((packed, before))
    summed = lax.psum_scatter(packed, "heads", scatter_dimension=0, tiled=True)
    summed = summed.astype(jnp.float32)
    whole = summed[:own_width].T
    mean_first = summed[own_width][:, None]
    mean_second = summed[own_width + 1][:, None]
    own_normed = (share_rows.astype(jnp.float32) - mean) * inverse
    own_grad = inverse * (whole - mean_first - own_normed * mean_second)
    grad_in = (grad_share.astype(jnp.float32) + own_grad).astype(jnp.bfloat16)
    return (grad_in, weight_grads, before)


def exchange_grads(weight_grads):
    members = lax.axis_size("seq")
    blocks = weight_grads.reshape(members, -1, weight_grads.shape[1])
    shares = lax.all_to_all(blocks, "seq", split_axis=0, concat_axis=0, tiled=True)
    return jnp.sum(shares.astype(jnp.float32), axis=0)


def split_grads(summed, own_width):
    summed = summed.reshape(-1, 4, own_width)
    return (jnp.swapaxes(summed[:, :3], 0, 1), summed[:, 3].T)


def shards(
    frames,
    qkv_spatial,
    out_spatial,
    qkv_temporal,
    out_temporal,
    spatial_mask,
    temporal_mask,
    cotangent,
):
    length = frames.shape[1]
    own_width = frames.shape[2]
    frame_count = temporal_mask.shape[1]
    local_count = length // lax.axis_size("seq")
    block_count = spatial_mask.shape[1]
    block_size = length // block_count
    grid_mask = (
        jnp.broadcast_to(
            spatial_mask[0][:, None, :, None], (block_count, block_size, block_count, block_size)
        ).reshape(length, length)
        == 1
    )
    block_ids = jnp.arange(length) // block_size
    spatial_allowed = (grid_mask | (block_ids[:, None] == block_ids[None, :]))[None]
    positions = lax.axis_index("seq") * local_count + jnp.arange(local_count)
    chosen = (positions // block_size)[:, None] == jnp.arange(block_count)[None, :]
    picked = jnp.sum(jnp.where(chosen[:, :, None, None], temporal_mask[None], 0), axis=1)
    frame_ids = jnp.arange(frame_count)
    causal = (frame_ids[:, None] >= frame_ids[None, :])[None]
    diagonal = (frame_ids[:, None] == frame_ids[None, :])[None]
    temporal_allowed = causal & ((picked == 1) | diagonal)
    frame_share = frames.reshape(length, own_width)
    cotangent_share = cotangent.reshape(length, own_width)
    frame_rows = row_features(frame_share)
    cotangent_share, frame_rows = lax.optimization_barrier((cotangent_share, frame_rows))
    half = length // 2
    early_rows = row_features(cotangent_share[:half])
    update, spatial_state = layer_forward(
        frame_share, frame_rows, qkv_spatial, out_spatial, spatial_allowed, length, 1
    )
    update, early_rows = lax.optimization_barrier((update, early_rows))
    hidden = add_update(frame_share, update)
    late_cotangent, hidden = lax.optimization_barrier((cotangent_share[half:], hidden))
    late_rows = row_features(late_cotangent)
    cotangent_rows = jnp.concatenate([early_rows, late_rows])
    position_share = relayout(hidden.reshape(1, length, own_width)).reshape(length, own_width)
    position_rows = row_features(position_share)
    late_update, temporal_state = layer_forward(
        position_share,
        position_rows,
        qkv_temporal,
        out_temporal,
        temporal_allowed,
        frame_count,
        local_count,
    )
    grad_position, temporal_grads, _ = layer_backward(
        position_share,
        cotangent_share,
        cotangent_rows,
        qkv_temporal,
        out_temporal,
        temporal_allowed,
        temporal_state,
    )
    temporal_sums = exchange_grads(temporal_grads)
    grad_position, temporal_sums = lax.optimization_barrier((grad_position, temporal_sums))
    hidden_grad = relayout(grad_position.reshape(1, length, own_width)).reshape(length, own_width)
    hidden_grad_rows = row_features(hidden_grad)
    late_update, hidden_grad_rows = lax.optimization_barrier((late_update, hidden_grad_rows))
    result = add_update(position_share, late_update)
    frames_grad, spatial_grads, early = layer_backward(
        frame_share,
        hidden_grad,
        hidden_grad_rows,
        qkv_spatial,
        out_spatial,
        spatial_allowed,
        spatial_state,
        result,
    )
    result = early
    reduced = split_grads(exchange_grads(spatial_grads), own_width) + split_grads(
        temporal_sums, own_width
    )
    return (
        result.reshape(frame_count, local_count, own_width),
        frames_grad.reshape(1, length, own_width),
        reduced[0],
        reduced[1],
        reduced[2],
        reduced[3],
    )


def solution(mesh):
    placed = (
        P("seq", None, "heads"),
        P(None, None, "heads"),
        P("heads", None),
        P(None, None, "heads"),
        P("heads", None),
        P("seq", None, None),
        P(),
        P(None, "seq", "heads"),
    )
    return jax.shard_map(
        shards,
        mesh=mesh,
        in_specs=placed,
        out_specs=(
            P(None, "seq", "heads"),
            P("seq", None, "heads"),
            P(None, "seq", "heads"),
            P("heads", "seq"),
            P(None, "seq", "heads"),
            P("heads", "seq"),
        ),
        check_vma=False,
    )
```
